256 devices in a mesh: state: 32 (over z, x_hi, core), seq: 8 (over y, x_lo).
Axes of the slice: x: 4 (x_hi: 2, x_lo: 2; x = x_hi * 2 + x_lo), y: 4, z: 8, core: 2. Of those that a mesh axis runs over, the one named last changes fastest.
Arguments:
- feature_u: bfloat16 [65536, 4096], P('state', 'seq'), may hold values from 0.0001 to 25000, as said below
- feature_v: bfloat16 [65536, 4096], P('state', 'seq'), may hold values from 0.0001 to 25000, as said below
- emission: bfloat16 [10240, 65536], P('seq', 'state'), may hold values from 0.099609375 to 10
- word_ids: int32 [64, 4], replicated, may hold values from 0 to 10239
- scales: float32 [64, 4], P('seq'), may hold values from 1 to 4
- backward_end: float32 [64, 65536], P('seq', 'state'), may hold values from 0.25 to 4
Outputs:
- backward_messages: float32 [4, 64, 65536], P(None, 'seq', 'state')
The draws below stay inside these ranges and needn't reach their ends.
Inputs may be any that keep to these rules, and one draw needn't show every extreme that they name: `feature_u`: positive transition features. `feature_v`: positive transition features.
All inputs are finite; a program needn't handle non-finite values.
Results may differ from the reference program's by a relative error of at most 0.0022.
Values may be sent and summed in bfloat16 or wider, within the bound.
A program may use at most 64 MiB of HBM per device.

```python
import math
import jax
import jax.numpy as jnp
import numpy as np
from jax import lax

STATES = 65536
RANK = 4096
VOCAB = 10240
STEPS = 4
SEQS = 64
N_STATE = 32


def heavy_values(key, shape, power):
    uniform_draw = jax.random.uniform(key, shape, minval=1e-06, maxval=1.0)
    tail = jnp.minimum(-jnp.log(uniform_draw), 12.0)
    return jnp.exp(power * tail - 9.0)


def draw_feature_u(key, part):
    key = jax.random.fold_in(key, 5)
    first_key, second_key = jax.random.split(key)
    power = 1.25
    spread = jnp.exp(jax.random.uniform(second_key, (1, RANK), minval=0.0, maxval=jnp.log(10.0)))
    return (heavy_values(first_key, (STATES, RANK), power) * spread).astype(jnp.bfloat16)


def draw_feature_v(key, part):
    key = jax.random.fold_in(key, 7)
    first_key, second_key = jax.random.split(key)
    power = 1.25
    spread = jnp.exp(jax.random.uniform(second_key, (STATES, 1), minval=0.0, maxval=jnp.log(10.0)))
    return (heavy_values(first_key, (STATES, RANK), power) * spread).astype(jnp.bfloat16)


def touch_ends(values, stream_key, low, largest):
    spot = [jax.random.randint(jax.random.fold_in(stream_key, axis), (), 0, length) for axis, length in enumerate(values.shape)]
    main_axis = values.shape.index(max(values.shape))
    next_to = spot[:main_axis] + [(spot[main_axis] + 1) % values.shape[main_axis]] + spot[main_axis + 1:]
    return values.at[tuple(spot)].set(low).at[tuple(next_to)].set(largest)


def shard_levels(key, extent, cuts, least, largest):
    def one(dim, parts):
        heights = jax.random.uniform(jax.random.fold_in(jax.random.fold_in(key, 6), dim), (parts,), jnp.float32, least / len(cuts), largest / len(cuts))
        return jnp.repeat(jnp.exp(heights), extent[dim] // parts).reshape((-1,) + (1,) * (len(extent) - dim - 1))

    factor_of = one(*cuts[0])
    for cut in cuts[1:]:
        factor_of = factor_of * one(*cut)
    return factor_of


def rank_bounds(amount, slope):
    loads = [(1 << 20) // math.isqrt(rank ** slope) + 1 for rank in range(1, amount + 1)]
    width = 1 + sum(loads) // (1 << 30)
    return np.cumsum(np.array([max(1, weight // width) for weight in loads]))


def ranked_ids(rng, dims, amount, skew):
    table = rank_bounds(amount, skew)
    ticket = jax.random.randint(jax.random.fold_in(rng, 1), dims, 0, int(table[amount - 1]))
    standing = jnp.searchsorted(jnp.asarray(table, jnp.int32), ticket, side="right")
    return jax.random.permutation(jax.random.fold_in(rng, 2), amount)[standing].astype(jnp.int32)


def setup_inputs(seed: int = 0) -> dict:
    arg_keys = jax.random.split(jax.random.key(seed), 7)
    feature_u = draw_feature_u(jax.random.fold_in(arg_keys[6], 71), 0)
    feature_v = draw_feature_v(jax.random.fold_in(arg_keys[6], 71), 0)
    emission = jnp.clip(jnp.exp(math.log(10.0) - 4.609084 * jax.random.uniform(arg_keys[2], (VOCAB, STATES), jnp.float32) ** shard_levels(arg_keys[2], (VOCAB, STATES), ((0, 8), (1, 32)), -0.2, 0.2)), 0.099609375, 10.0).astype(jnp.bfloat16)
    word_ids = touch_ends(ranked_ids(arg_keys[3], (SEQS, STEPS), VOCAB, 2), jax.random.fold_in(arg_keys[3], 3), 0, VOCAB - 1).astype(jnp.int32)
    scales = jnp.clip(jnp.exp(math.log(4.0) - 1.3862944 * jax.random.uniform(arg_keys[4], (SEQS, STEPS), jnp.float32) ** shard_levels(arg_keys[4], (SEQS, STEPS), ((0, 8),), -0.2, 0.2)), 1.0, 4.0)
    backward_end = jnp.clip(jnp.exp(math.log(4.0) - 2.7725887 * jax.random.uniform(arg_keys[5], (SEQS, STATES), jnp.float32) ** shard_levels(arg_keys[5], (SEQS, STATES), ((0, 8), (1, 32)), -0.2, 0.2)), 0.25, 4.0)
    return dict(feature_u=feature_u, feature_v=feature_v, emission=emission, word_ids=word_ids, scales=scales, backward_end=backward_end)


def reference(feature_u, feature_v, emission, word_ids, scales, backward_end):
    column_mass = jnp.sum(feature_v, axis=0, dtype=jnp.float32)
    blocks = feature_u.reshape(N_STATE, STATES // N_STATE, RANK)

    def block_norm(block):
        return jnp.dot(block.astype(jnp.float32), column_mass, precision=lax.Precision.HIGHEST)

    row_norm = lax.map(block_norm, blocks).reshape(STATES)
    picked = jnp.take(emission, word_ids, axis=0)
    current = backward_end
    results = []
    for position in reversed(range(STEPS)):
        weighted = (picked[:, position, :].astype(jnp.float32) * current).astype(jnp.bfloat16)
        message = jnp.dot(weighted, feature_v, preferred_element_type=jnp.float32).astype(jnp.bfloat16)
        unscaled = lax.dot_general(message, feature_u, (((1,), (1,)), ((), ())), preferred_element_type=jnp.float32)
        current = unscaled / (row_norm[None, :] * scales[:, position:position + 1])
        results.insert(0, current)
    return jnp.stack(results)
```

```python
import jax
import jax.numpy as jnp
from jax import lax
from jax.experimental import pallas as pl
from jax.experimental.pallas import tpu as pltpu
from jax.sharding import PartitionSpec as P

CHAINS = 1
STATES = 2048
RANK = 512
SEQS = 64
STEPS = 4
N_SEQ = 8
N_STATE = 32
BLOCK = STATES // N_SEQ
TILES = 16
ROWS = SEQS // CHAINS
HALF = TILES // CHAINS
BF = jnp.bfloat16
F32 = jnp.float32


def kernel(
    u_hbm, v_hbm, em_hbm, ids_hbm, sc_hbm, be_hbm, out_hbm,
    u, v, em, ids, sc, be,
    scs, ends, csbuf, nsend, nrecv,
    emsend, emrecv, wbuf, part, arr, red, msg, rsend, rrecv, rown, bk,
    load_sem, init_send, init_recv, sc_recv, cs_send, cs_recv, n_send, n_recv,
    em_send, em_recv, ag_send, ag_recv, ar_send, ar_recv, red_send, msg_recv,
    rs_send, rs_recv, out_send, out_recv, out_local,
):
    my_state = lax.axis_index("state")
    my_seq = lax.axis_index("seq")

    def peer(d):
        return lax.rem(my_seq + d, N_SEQ)

    def remote(src, dst, send, recv, state, seq):
        return pltpu.make_async_remote_copy(
            src_ref=src, dst_ref=dst, send_sem=send, recv_sem=recv,
            device_id={"state": state, "seq": seq},
            device_id_type=pl.DeviceIdType.MESH,
        )

    def wait(ref, sem):
        pltpu.make_async_copy(ref, ref, sem).wait()

    loads = [
        pltpu.make_async_copy(src, dst, load_sem.at[i])
        for i, (src, dst) in enumerate(
            ((ids_hbm, ids), (em_hbm, em), (be_hbm, be), (sc_hbm, sc), (v_hbm, v), (u_hbm, u))
        )
    ]
    for load in loads:
        load.start()

    barrier = pltpu.get_barrier_semaphore()
    for d in range(1, N_SEQ):
        pl.semaphore_signal(
            barrier, inc=1, device_id={"state": my_state, "seq": peer(d)},
            device_id_type=pl.DeviceIdType.MESH,
        )

    @pl.loop(1, N_STATE)
    def _(d):
        pl.semaphore_signal(
            barrier, inc=1,
            device_id={"state": lax.rem(my_state + d, N_STATE), "seq": my_seq},
            device_id_type=pl.DeviceIdType.MESH,
        )

    def block_of(k):
        return pl.ds(pl.multiple_of(k * BLOCK, BLOCK), BLOCK)

    def column(values, step):
        lane = lax.broadcasted_iota(jnp.int32, values.shape, 1)
        return jnp.sum(
            jnp.where(lane == STEPS - 1 - step, values.astype(F32), 0.0), axis=1, keepdims=True
        )

    table_rows = em.shape[0]

    def onehot(step):
        wanted = column(ids[...], step) - (my_seq * table_rows).astype(F32)
        word = lax.broadcasted_iota(jnp.int32, (SEQS, table_rows), 1).astype(F32)
        return jnp.where(word == wanted, 1.0, 0.0).astype(BF)

    def pick_send(step):
        hot = onehot(step)
        for d in list(range(1, N_SEQ)) + [0]:
            k = peer(d)
            rows = jnp.dot(hot, em[:, block_of(k)], preferred_element_type=F32).astype(BF)
            if d == 0:
                emrecv[my_seq] = rows
            else:
                emsend[k] = rows
                remote(
                    emsend.at[k], emrecv.at[my_seq], em_send, em_recv, my_state, k
                ).start()

    def pick_wait():
        wait(emrecv.at[pl.ds(0, N_SEQ - 1)], em_recv)
        wait(emsend.at[pl.ds(0, N_SEQ - 1)], em_send)

    def rows_of(c):
        return pl.ds(c * ROWS, ROWS)

    def gather_send(c, current):
        rows = rows_of(c)
        picked = jnp.sum(emrecv[:, rows, :].astype(F32), axis=0)
        wbuf[my_seq, rows, :] = (picked * current).astype(BF)
        for d in range(1, N_SEQ):
            remote(
                wbuf.at[my_seq, rows], wbuf.at[my_seq, rows], ag_send.at[c], ag_recv.at[c, my_seq],
                my_state, peer(d),
            ).start()

    loads[0].wait()
    loads[1].wait()
    loads[2].wait()
    loads[3].wait()
    pl.semaphore_wait(barrier, N_SEQ - 1 + N_STATE - 1)
    ends[my_seq] = be[:, block_of(my_seq)]
    scs[my_seq] = sc[...]
    for d in range(1, N_SEQ):
        k = peer(d)
        remote(
            be.at[:, block_of(k)], ends.at[my_seq], init_send, init_recv, my_state, k
        ).start()
        remote(scs.at[my_seq], scs.at[my_seq], cs_send.at[1], sc_recv, my_state, k).start()
    pick_send(0)

    loads[4].wait()
    sums = jnp.dot(jnp.ones((16, STATES), BF), v[...], preferred_element_type=F32)[0:1]
    csbuf[my_state] = jnp.concatenate(
        [sums[:, i * 128 : (i + 1) * 128] for i in range(4)] + [jnp.zeros((4, 128), F32)], axis=0
    )

    @pl.loop(1, N_STATE)
    def _(d):
        remote(
            csbuf.at[my_state], csbuf.at[my_state], cs_send.at[0], cs_recv,
            lax.rem(my_state + d, N_STATE), my_seq,
        ).start()

    pick_wait()
    wait(ends.at[pl.ds(0, N_SEQ - 1)], init_recv)
    wait(scs.at[pl.ds(0, N_SEQ - 1)], sc_recv)
    first = ends[...].reshape(SEQS, BLOCK)
    for c in range(CHAINS):
        gather_send(c, first[c * ROWS : (c + 1) * ROWS])

    loads[5].wait()
    wait(csbuf.at[pl.ds(0, N_STATE - 1)], cs_recv)
    mass = jnp.sum(csbuf[...], axis=0)
    mass = jnp.concatenate([mass[i : i + 1] for i in range(4)], axis=1)
    hi = mass.astype(BF).astype(F32)
    mid = (mass - hi).astype(BF).astype(F32)
    low = mass - hi - mid
    parts = jnp.concatenate([hi, mid, low, jnp.zeros((13, RANK), F32)], axis=0).astype(BF)
    for d in list(range(1, N_SEQ)) + [0]:
        k = peer(d)
        norm = lax.dot_general(
            parts, u[block_of(k), :], (((1,), (1,)), ((), ())), preferred_element_type=F32
        )[0:8]
        if d == 0:
            nrecv[my_seq] = norm
        else:
            nsend[k] = norm
            remote(nsend.at[k], nrecv.at[my_seq], n_send, n_recv, my_state, k).start()

    def first_matmul(c):
        rows = rows_of(c)
        acc = None
        for d in range(N_SEQ):
            k = peer(d)
            if d:
                wait(wbuf.at[k, rows], ag_recv.at[c, k])
            term = jnp.dot(wbuf[k, rows, :], v[block_of(k), :], preferred_element_type=F32)
            acc = term if acc is None else acc + term
        wait(wbuf.at[pl.ds(0, N_SEQ - 1), rows], ag_send.at[c])
        for i in range(HALF):
            r, l = divmod(i, 4)
            part[c * HALF + i] = acc[r * 16 : r * 16 + 16, l * 128 : l * 128 + 128].astype(BF)
        for i in range(HALF):
            tile = c * HALF + i
            owner = 2 * tile + tile % 2

            @pl.when(owner == my_state)
            def _():
                arr[my_state] = part[tile]

            @pl.when(owner != my_state)
            def _():
                remote(
                    part.at[tile], arr.at[my_state], ar_send.at[c], ar_recv, owner, my_seq
                ).start()

    chip = my_state // 2
    is_owner = lax.rem(my_state, 2) == lax.rem(chip, 2)

    def reduce_tile(c):
        @pl.when(jnp.logical_and(is_owner, chip // HALF == c))
        def _():
            wait(arr.at[pl.ds(0, N_STATE - 1)], ar_recv)
            red[...] = jnp.sum(arr[...].astype(F32), axis=0).astype(BF)
            pltpu.make_async_copy(red, msg.at[chip], msg_recv.at[c]).start()

            @pl.loop(1, N_STATE)
            def _(d):
                remote(
                    red, msg.at[chip], red_send, msg_recv.at[c],
                    lax.rem(my_state + d, N_STATE), my_seq,
                ).start()

    def second_matmul(c):
        rows = rows_of(c)
        tiles = pl.ds(c * HALF, HALF)
        wait(msg.at[tiles], msg_recv.at[c])
        m = jnp.concatenate(
            [
                jnp.concatenate([msg[c * HALF + r * 4 + l] for l in range(4)], axis=1)
                for r in range(HALF // 4)
            ],
            axis=0,
        )
        for d in list(range(1, N_SEQ)) + [0]:
            k = peer(d)
            block = lax.dot_general(
                m, u[block_of(k), :], (((1,), (1,)), ((), ())), preferred_element_type=F32
            )
            if d == 0:
                rown[rows, :] = block
            else:
                rsend[k, rows, :] = block.astype(BF)
                remote(
                    rsend.at[k, rows], rrecv.at[d - 1, rows], rs_send.at[c], rs_recv.at[c],
                    my_state, k,
                ).start()

        @pl.when(jnp.logical_and(is_owner, chip // HALF == c))
        def _():
            wait(arr.at[pl.ds(0, N_STATE - 1)], red_send)
            wait(part.at[pl.ds(0, HALF - 1)], ar_send.at[c])

        @pl.when(jnp.logical_not(jnp.logical_and(is_owner, chip // HALF == c)))
        def _():
            wait(part.at[pl.ds(0, HALF)], ar_send.at[c])

    def finish(c, step, norm):
        rows = rows_of(c)
        wait(rrecv.at[:, rows], rs_recv.at[c])
        wait(rsend.at[pl.ds(0, N_SEQ - 1), rows], rs_send.at[c])
        total = rown[rows, :] + jnp.sum(rrecv[:, rows, :].astype(F32), axis=0)
        scale = scale_column(step)[c * ROWS : (c + 1) * ROWS]
        current = total / (norm * scale)
        return current

    def scale_column(step):
        return column(scs[...].reshape(SEQS, STEPS), step)

    def step_body(step):
        for c in range(CHAINS):
            first_matmul(c)

        @pl.when(step < STEPS - 1)
        def _():
            pick_send(step + 1)

        for c in range(CHAINS):
            reduce_tile(c)
        for c in range(CHAINS):
            second_matmul(c)

        @pl.when(step == 0)
        def _():
            wait(nrecv.at[pl.ds(0, N_SEQ - 1)], n_recv)
            nrecv[0, 0:1, :] = jnp.sum(jnp.sum(nrecv[...], axis=0), axis=0, keepdims=True)

        @pl.when(step > 0)
        def _():
            wait(bk.at[pl.ds(0, SEQS - 8)], out_send)
            wait(bk.at[pl.ds(0, 8)], out_local)

        @pl.when(step < STEPS - 1)
        def _():
            pick_wait()

        norm = nrecv[0, 0:1, :]
        for c in range(CHAINS):
            current = finish(c, step, norm)
            bk[rows_of(c), :] = current

            @pl.when(step < STEPS - 1)
            def _():
                gather_send(c, current)

        for d in range(N_SEQ):
            k = peer(d)
            src = bk.at[pl.ds(pl.multiple_of(k * 8, 8), 8)]
            dst = out_hbm.at[STEPS - 1 - step, :, block_of(my_seq)]
            if d == 0:
                pltpu.make_async_copy(src, dst, out_local).start()
            else:
                remote(src, dst, out_send, out_recv, my_state, k).start()

    pl.loop(0, STEPS)(step_body)

    wait(bk.at[pl.ds(0, SEQS - 8)], out_send)
    wait(bk.at[pl.ds(0, 8)], out_local)
    wait(out_hbm.at[:, :, pl.ds(0, STATES - BLOCK)], out_recv)
    wait(ends.at[pl.ds(0, N_SEQ - 1)], init_send)
    wait(scs.at[pl.ds(0, N_SEQ - 1)], cs_send.at[1])
    wait(csbuf.at[pl.ds(0, N_STATE - 1)], cs_send.at[0])
    wait(nsend.at[pl.ds(0, N_SEQ - 1)], n_send)


def body(feature_u, feature_v, emission, word_ids, scales, backward_end):
    dma = pltpu.SemaphoreType.DMA
    scratch = [
        pltpu.VMEM(feature_u.shape, BF),
        pltpu.VMEM(feature_v.shape, BF),
        pltpu.VMEM(emission.shape, BF),
        pltpu.VMEM(word_ids.shape, jnp.int32),
        pltpu.VMEM(scales.shape, F32),
        pltpu.VMEM(backward_end.shape, F32),
        pltpu.VMEM((N_SEQ, 8, STEPS), F32),
        pltpu.VMEM((N_SEQ, 8, BLOCK), F32),
        pltpu.VMEM((N_STATE, 8, 128), F32),
        pltpu.VMEM((N_SEQ, 8, BLOCK), F32),
        pltpu.VMEM((N_SEQ, 8, BLOCK), F32),
        pltpu.VMEM((N_SEQ, SEQS, BLOCK), BF),
        pltpu.VMEM((N_SEQ, SEQS, BLOCK), BF),
        pltpu.VMEM((N_SEQ, SEQS, BLOCK), BF),
        pltpu.VMEM((TILES, 16, 128), BF),
        pltpu.VMEM((N_STATE, 16, 128), BF),
        pltpu.VMEM((16, 128), BF),
        pltpu.VMEM((TILES, 16, 128), BF),
        pltpu.VMEM((N_SEQ, SEQS, BLOCK), BF),
        pltpu.VMEM((N_SEQ - 1, SEQS, BLOCK), BF),
        pltpu.VMEM((SEQS, BLOCK), F32),
        pltpu.VMEM((SEQS, BLOCK), F32),
        dma((6,)), dma, dma, dma, dma((2,)), dma, dma, dma,
        dma, dma, dma((CHAINS,)), dma((CHAINS, N_SEQ)), dma((CHAINS,)), dma, dma, dma((CHAINS,)),
        dma((CHAINS,)), dma((CHAINS,)), dma, dma, dma,
    ]
    return pl.pallas_call(
        kernel,
        out_shape=jax.ShapeDtypeStruct((STEPS, 8, STATES), F32),
        in_specs=[pl.BlockSpec(memory_space=pl.ANY)] * 6,
        out_specs=pl.BlockSpec(memory_space=pl.ANY),
        scratch_shapes=scratch,
        compiler_params=pltpu.CompilerParams(
            collective_id=0, has_side_effects=True, vmem_limit_bytes=40 * 2**20
        ),
        name="backward_messages",
    )(feature_u, feature_v, emission, word_ids, scales, backward_end)


def solution(mesh):
    placed = (
        P("state", "seq"),
        P("state", "seq"),
        P("seq", "state"),
        P(),
        P("seq", None),
        P("seq", "state"),
    )
    return jax.shard_map(
        body, mesh=mesh, in_specs=placed, out_specs=P(None, "seq", "state"), check_vma=False
    )
```

```python
import jax
import jax.numpy as jnp
from jax import lax
from jax.experimental import pallas as pl
from jax.experimental.pallas import tpu as pltpu
from jax.sharding import PartitionSpec as P

CHAINS = 2
STATES = 2048
RANK = 512
SEQS = 64
STEPS = 4
N_SEQ = 8
N_Z = 8
PLANE = 4
BLOCK = STATES // N_SEQ
LANES = RANK // PLANE
ROWS = SEQS // CHAINS
HOME = SEQS // N_SEQ
BF = jnp.bfloat16
F32 = jnp.float32
PLANE_TYPE = F32
SEQ_ORDER = ((2, 1), (2, 0), (1, 1), (3, 1), (1, 0), (3, 0), (0, 1))
Z_ORDER = (4, 3, 5, 2, 6, 1, 7)
PLANE_ORDER = ((1, 0), (1, 1), (0, 1))
PEERS = len(SEQ_ORDER) + len(Z_ORDER) + len(PLANE_ORDER)


def kernel(
    u_hbm, v_hbm, em_hbm, ids_hbm, sc_hbm, be_hbm, out_hbm,
    u, v, em, ids, sc, be, square, words, scale_own,
    init_out, init_in, mass_own, mass_plane, mass_z, norm_out, norm_in, norm_all,
    pick_out, pick_in, gather_in, gather_own, plane_out, plane_in, z_in, message_in,
    scatter_out, scatter_in, scatter_own, backward, last_out, last_in, last_result,
    load_sem, em_sem, init_sem, mass_sem, norm_sem, norm_all_sem, pick_sem,
    gather_send, gather_recv, plane_sem, z_sem, message_sem, scatter_sem, out_sem, out_local, last_sem,
):
    my_state = lax.axis_index("state")
    my_seq = lax.axis_index("seq")
    my_z, my_q = my_state // PLANE, lax.rem(my_state, PLANE)
    my_xh, my_core = my_q // 2, lax.rem(my_q, 2)
    my_y, my_xl = my_seq // 2, lax.rem(my_seq, 2)

    def flip(x, d):
        return 1 - x if d else x

    def seq_to(i):
        dy, dx = SEQ_ORDER[i]
        return lax.rem(my_y + dy, 4) * 2 + flip(my_xl, dx)

    def seq_from(i):
        dy, dx = SEQ_ORDER[i]
        return lax.rem(my_y + 4 - dy, 4) * 2 + flip(my_xl, dx)

    def plane_to(i):
        dx, dc = PLANE_ORDER[i]
        return flip(my_xh, dx) * 2 + flip(my_core, dc)

    def remote(src, dst, send, recv, state, seq):
        pltpu.make_async_remote_copy(
            src_ref=src, dst_ref=dst, send_sem=send, recv_sem=recv,
            device_id={"state": state, "seq": seq},
            device_id_type=pl.DeviceIdType.MESH,
        ).start()

    def to_seq(i, src, dst, sems):
        remote(src, dst, sems[0], sems[1], my_state, seq_to(i))

    def to_z(d, src, dst, sems):
        remote(src, dst, sems[0], sems[1], lax.rem(my_z + d, N_Z) * PLANE + my_q, my_seq)

    def to_plane(i, src, dst, sems):
        remote(src, dst, sems[0], sems[1], my_z * PLANE + plane_to(i), my_seq)

    def pair(ref, *index):
        return ref.at[(0,) + index], ref.at[(1,) + index]

    def wait(ref, sem):
        pltpu.make_async_copy(ref, ref, sem).wait()

    def block_of(k):
        return pl.ds(pl.multiple_of(k * BLOCK, BLOCK), BLOCK)

    def rows_of(c):
        return pl.ds(c * ROWS, ROWS)

    small = [
        pltpu.make_async_copy(src, dst, load_sem.at[i])
        for i, (src, dst) in enumerate(((ids_hbm, ids), (sc_hbm, sc), (be_hbm, be)))
    ]
    for load in small:
        load.start()
    em_loads = []
    for i in range(N_SEQ):
        k = seq_to(i) if i < N_SEQ - 1 else my_seq
        em_loads.append(
            pltpu.make_async_copy(em_hbm.at[:, block_of(k)], em.at[:, block_of(k)], em_sem.at[i])
        )
    for load in em_loads:
        load.start()
    v_load = pltpu.make_async_copy(v_hbm, v, load_sem.at[3])
    u_load = pltpu.make_async_copy(u_hbm, u, load_sem.at[4])
    v_load.start()
    u_load.start()

    barrier = pltpu.get_barrier_semaphore()

    def greet(state, seq):
        pl.semaphore_signal(
            barrier, inc=1, device_id={"state": state, "seq": seq},
            device_id_type=pl.DeviceIdType.MESH,
        )

    for d in Z_ORDER:
        greet(lax.rem(my_z + d, N_Z) * PLANE + my_q, my_seq)
    for i in range(len(SEQ_ORDER)):
        greet(my_state, seq_to(i))
    for i in range(len(PLANE_ORDER)):
        greet(my_z * PLANE + plane_to(i), my_seq)

    def columns(ref, height, width):
        square[...] = jnp.zeros_like(square)
        square[0:height, 0:width] = ref[...].astype(F32)
        return jnp.transpose(square[...])

    def column(values, step):
        lane = lax.broadcasted_iota(jnp.int32, values.shape, 1)
        return jnp.sum(jnp.where(lane == STEPS - 1 - step, values, 0.0), axis=1, keepdims=True)

    small[0].wait()
    words[...] = columns(ids, STEPS, SEQS)[0:SEQS]
    small[1].wait()
    scale_own[...] = columns(sc, STEPS, HOME)[0:HOME]
    table_rows = em.shape[0]

    def onehot(step):
        wanted = column(words[...], step) - (my_seq * table_rows).astype(F32)
        word = lax.broadcasted_iota(jnp.int32, (SEQS, table_rows), 1).astype(F32)
        return jnp.where(word == wanted, 1.0, 0.0).astype(BF)

    def pick(step, before=None):
        hot = onehot(step)
        for i in range(N_SEQ):
            k = seq_to(i) if i < N_SEQ - 1 else my_seq
            if before is not None:
                before(i)
            rows = jnp.dot(hot, em[:, block_of(k)], preferred_element_type=F32).astype(BF)
            if i == N_SEQ - 1:
                pick_in[i] = rows
            else:
                pick_out[i] = rows
                to_seq(i, pick_out.at[i], pick_in.at[i], pair(pick_sem))

    def pick_wait():
        wait(pick_in.at[pl.ds(0, N_SEQ - 1)], pick_sem.at[1])
        wait(pick_out, pick_sem.at[0])

    small[2].wait()
    for i in range(N_SEQ):
        k = seq_to(i) if i < N_SEQ - 1 else my_seq
        init_out[i, :, 0:BLOCK] = be[:, block_of(k)]
        init_out[i, :, BLOCK : BLOCK + 128] = scale_own[...]
    pl.semaphore_wait(barrier, PEERS)
    for i in range(N_SEQ - 1):
        to_seq(i, init_out.at[i], init_in.at[my_seq], pair(init_sem))
    init_in[my_seq] = init_out[N_SEQ - 1]
    pick(0, before=lambda i: em_loads[i].wait())

    v_load.wait()
    sums = jnp.dot(jnp.ones((16, STATES), BF), v[...], preferred_element_type=F32)[0:1]
    mass_own[...] = jnp.concatenate(
        [sums[:, i * 128 : (i + 1) * 128] for i in range(4)] + [jnp.zeros((4, 128), F32)], axis=0
    )
    mass_plane[3] = mass_own[...]
    for i in range(PLANE - 1):
        to_plane(i, mass_own, mass_plane.at[i], pair(mass_sem, 0))

    def send_weighted(c, current):
        rows = rows_of(c)
        picked = jnp.sum(pick_in[:, rows, :].astype(F32), axis=0)
        gather_own[rows, :] = (picked * current).astype(BF)
        for i in range(N_SEQ - 1):
            to_seq(
                i, gather_own.at[rows], gather_in.at[i, rows],
                (gather_send.at[c], gather_recv.at[c, i]),
            )

    wait(init_in.at[pl.ds(0, N_SEQ - 1)], init_sem.at[1])
    pick_wait()
    first = init_in[:, :, 0:BLOCK].reshape(SEQS, BLOCK)
    for c in range(CHAINS):
        send_weighted(c, first[c * ROWS : (c + 1) * ROWS])

    wait(mass_plane.at[pl.ds(0, 3)], mass_sem.at[1, 0])
    mass_z[my_z] = jnp.sum(mass_plane[...], axis=0)
    for d in Z_ORDER:
        to_z(d, mass_z.at[my_z], mass_z.at[my_z], pair(mass_sem, 1))

    def first_matmul(c):
        rows = rows_of(c)
        acc = jnp.dot(gather_own[rows, :], v[block_of(my_seq), :], preferred_element_type=F32)
        for i in reversed(range(N_SEQ - 1)):
            wait(gather_in.at[i, rows], gather_recv.at[c, i])
            acc += jnp.dot(
                gather_in[i, rows, :], v[block_of(seq_from(i)), :], preferred_element_type=F32
            )
        for q in range(PLANE):
            plane_out[q, rows, :] = acc[:, q * LANES : (q + 1) * LANES].astype(PLANE_TYPE)
        for i in range(PLANE - 1):
            to_plane(
                i, plane_out.at[plane_to(i), rows], plane_in.at[i, rows], pair(plane_sem, c)
            )
        wait(gather_in.at[pl.ds(0, N_SEQ - 1), rows], gather_send.at[c])

    def sum_plane(c, turn):
        rows = rows_of(c)
        wait(plane_in.at[:, rows], plane_sem.at[1, c])
        total = plane_out[my_q, rows, :].astype(F32)
        total += jnp.sum(plane_in[:, rows, :].astype(F32), axis=0)
        z_in[turn, my_z, rows, :] = total.astype(BF)
        for d in Z_ORDER:
            block = z_in.at[turn, my_z, rows]
            to_z(d, block, block, pair(z_sem, c, turn))
        wait(plane_in.at[:, rows], plane_sem.at[0, c])

    def sum_z(c, turn):
        rows = rows_of(c)
        wait(z_in.at[turn, pl.ds(0, N_Z - 1), rows], z_sem.at[1, c, turn])
        message_in[my_q, rows, :] = jnp.sum(z_in[turn, :, rows, :].astype(F32), axis=0).astype(BF)
        for i in range(PLANE - 1):
            to_plane(
                i, message_in.at[my_q, rows], message_in.at[my_q, rows], pair(message_sem, c)
            )
        wait(z_in.at[turn, pl.ds(0, N_Z - 1), rows], z_sem.at[0, c, turn])

    def message(c):
        rows = rows_of(c)
        wait(message_in.at[pl.ds(0, PLANE - 1), rows], message_sem.at[1, c])
        return jnp.concatenate([message_in[q, rows, :] for q in range(PLANE)], axis=1)

    def message_sent(c):
        wait(message_in.at[pl.ds(0, PLANE - 1), rows_of(c)], message_sem.at[0, c])

    def expand(left, k):
        return lax.dot_general(
            left, u[block_of(k), :], (((1,), (1,)), ((), ())), preferred_element_type=F32
        )

    def second_matmul(c):
        rows = rows_of(c)
        left = message(c)
        for i in range(N_SEQ - 1):
            scatter_out[i, rows, :] = expand(left, seq_to(i)).astype(BF)
            to_seq(i, scatter_out.at[i, rows], scatter_in.at[i, rows], pair(scatter_sem, c))
        scatter_own[rows, :] = expand(left, my_seq)
        message_sent(c)

    def send_outputs(step):
        for i in range(N_SEQ - 1):
            src = backward.at[pl.ds(pl.multiple_of(seq_to(i) * HOME, HOME), HOME)]
            to_seq(i, src, out_hbm.at[STEPS - 1 - step, :, block_of(my_seq)], pair(out_sem))
        pltpu.make_async_copy(
            backward.at[pl.ds(pl.multiple_of(my_seq * HOME, HOME), HOME)],
            out_hbm.at[STEPS - 1 - step, :, block_of(my_seq)],
            out_local,
        ).start()

    def outputs_sent():
        wait(backward.at[pl.ds(0, SEQS - HOME)], out_sem.at[0])
        wait(backward.at[pl.ds(0, HOME)], out_local)

    def send_norm():
        wait(mass_z.at[pl.ds(0, N_Z - 1)], mass_sem.at[1, 1])
        mass = jnp.sum(mass_z[...], axis=0)
        mass = jnp.concatenate([mass[i : i + 1] for i in range(4)], axis=1)
        hi = mass.astype(BF).astype(F32)
        mid = (mass - hi).astype(BF).astype(F32)
        low = mass - hi - mid
        parts = jnp.concatenate([hi, mid, low, jnp.zeros((13, RANK), F32)], axis=0).astype(BF)
        for i in range(N_SEQ - 1):
            norm_out[i] = expand(parts, seq_to(i))[0:8]
            to_seq(i, norm_out.at[i], norm_in.at[i], pair(norm_sem))
        norm_in[N_SEQ - 1] = expand(parts, my_seq)[0:8]

    def finish_norm():
        wait(norm_in.at[pl.ds(0, N_SEQ - 1)], norm_sem.at[1])
        total = jnp.sum(jnp.sum(norm_in[...], axis=0), axis=0, keepdims=True)
        norm_all[my_seq] = jnp.broadcast_to(total, (8, BLOCK))
        for i in range(N_SEQ - 1):
            to_seq(i, norm_all.at[my_seq], norm_all.at[my_seq], pair(norm_all_sem))

    def step_body(step):
        turn = lax.rem(step, 2)
        for c in range(CHAINS):
            first_matmul(c)
        for c in range(CHAINS):
            sum_plane(c, turn)

        @pl.when(step == 0)
        def _():
            u_load.wait()
            send_norm()

        @pl.when(step > 0)
        def _():
            send_outputs(step - 1)

        pick(step + 1)
        for c in range(CHAINS):
            sum_z(c, turn)
        for c in range(CHAINS):
            second_matmul(c)

        @pl.when(step == 0)
        def _():
            finish_norm()

        @pl.when(step > 0)
        def _():
            outputs_sent()

        pick_wait()
        norm = norm_all[my_seq][0:1]
        scales = column(init_in[:, :, BLOCK : BLOCK + 128].reshape(SEQS, 128), step)
        for c in range(CHAINS):
            rows = rows_of(c)
            wait(scatter_in.at[:, rows], scatter_sem.at[1, c])
            total = scatter_own[rows, :] + jnp.sum(scatter_in[:, rows, :].astype(F32), axis=0)
            current = total / (norm * scales[c * ROWS : (c + 1) * ROWS])
            send_weighted(c, current)
            backward[rows, :] = current
            wait(scatter_out.at[:, rows], scatter_sem.at[0, c])

    pl.loop(0, STEPS - 1)(step_body)

    for c in range(CHAINS):
        first_matmul(c)
    for c in range(CHAINS):
        sum_plane(c, (STEPS - 1) % 2)
    send_outputs(STEPS - 2)
    for c in range(CHAINS):
        sum_z(c, (STEPS - 1) % 2)
    homes = N_SEQ // CHAINS
    for c in range(CHAINS):
        left = message(c)
        for n in range(N_SEQ // 2):
            low, high = expand(left, n), expand(left, n + N_SEQ // 2)
            for h in range(homes):
                part = slice(h * HOME, (h + 1) * HOME)
                both = jnp.concatenate([low[part], high[part]], axis=0)
                last_out[c * homes + h, :, n * BLOCK : (n + 1) * BLOCK] = both.astype(BF)
        for h in range(homes):
            home = c * homes + h

            @pl.when(home != my_seq)
            def _():
                remote(
                    last_out.at[home], last_in.at[my_seq], last_sem.at[0], last_sem.at[1],
                    my_state, home,
                )

            @pl.when(home == my_seq)
            def _():
                last_in[my_seq] = last_out[home]

        message_sent(c)

    wait(norm_all.at[pl.ds(0, N_SEQ - 1)], norm_all_sem.at[1])
    scale = column(scale_own[...], STEPS - 1)
    wait(last_in.at[pl.ds(0, N_SEQ - 1)], last_sem.at[1])
    total = jnp.sum(last_in[...].astype(F32), axis=0)
    for k in range(N_SEQ):
        r, l = divmod(k, N_SEQ // 2)
        block = total[r * HOME : (r + 1) * HOME, l * BLOCK : (l + 1) * BLOCK]
        last_result[:, k * BLOCK : (k + 1) * BLOCK] = block / (norm_all[k][0:1] * scale)
    result = pltpu.make_async_copy(last_result, out_hbm.at[0], load_sem.at[0])
    result.start()

    outputs_sent()
    wait(out_hbm.at[pl.ds(1, STEPS - 1), :, pl.ds(0, STATES - BLOCK)], out_sem.at[1])
    wait(init_in.at[pl.ds(0, N_SEQ - 1)], init_sem.at[0])
    wait(mass_plane.at[pl.ds(0, 3)], mass_sem.at[0, 0])
    wait(mass_z.at[pl.ds(0, N_Z - 1)], mass_sem.at[0, 1])
    wait(norm_out, norm_sem.at[0])
    wait(norm_all.at[pl.ds(0, N_SEQ - 1)], norm_all_sem.at[0])
    wait(last_in.at[pl.ds(0, N_SEQ - 1)], last_sem.at[0])
    result.wait()


def body(feature_u, feature_v, emission, word_ids, scales, backward_end):
    dma = pltpu.SemaphoreType.DMA
    word_ids, scales = word_ids.T, scales.T
    vm = pltpu.VMEM
    scratch = [
        vm(feature_u.shape, BF),
        vm(feature_v.shape, BF),
        vm(emission.shape, BF),
        vm(word_ids.shape, jnp.int32),
        vm(scales.shape, F32),
        vm(backward_end.shape, F32),
        vm((128, 128), F32),
        vm((SEQS, 128), F32),
        vm((HOME, 128), F32),
        vm((N_SEQ, HOME, BLOCK + 128), F32),
        vm((N_SEQ, HOME, BLOCK + 128), F32),
        vm((8, 128), F32),
        vm((4, 8, 128), F32),
        vm((N_Z, 8, 128), F32),
        vm((N_SEQ - 1, 8, BLOCK), F32),
        vm((N_SEQ, 8, BLOCK), F32),
        vm((N_SEQ, 8, BLOCK), F32),
        vm((N_SEQ - 1, SEQS, BLOCK), BF),
        vm((N_SEQ, SEQS, BLOCK), BF),
        vm((N_SEQ - 1, SEQS, BLOCK), BF),
        vm((SEQS, BLOCK), BF),
        vm((PLANE, SEQS, LANES), PLANE_TYPE),
        vm((PLANE - 1, SEQS, LANES), PLANE_TYPE),
        vm((2, N_Z, SEQS, LANES), BF),
        vm((PLANE, SEQS, LANES), BF),
        vm((N_SEQ - 1, SEQS, BLOCK), BF),
        vm((N_SEQ - 1, SEQS, BLOCK), BF),
        vm((SEQS, BLOCK), F32),
        vm((SEQS, BLOCK), F32),
        vm((N_SEQ, 2 * HOME, STATES // 2), BF),
        vm((N_SEQ, 2 * HOME, STATES // 2), BF),
        vm((HOME, STATES), F32),
        dma((5,)), dma((N_SEQ,)), dma((2,)), dma((2, 2)), dma((2,)), dma((2,)), dma((2,)),
        dma((CHAINS,)), dma((CHAINS, N_SEQ - 1)), dma((2, CHAINS)), dma((2, CHAINS, 2)),
        dma((2, CHAINS)), dma((2, CHAINS)), dma((2,)), dma, dma((2,)),
    ]
    return pl.pallas_call(
        kernel,
        out_shape=jax.ShapeDtypeStruct((STEPS, HOME, STATES), F32),
        in_specs=[pl.BlockSpec(memory_space=pl.ANY)] * 6,
        out_specs=pl.BlockSpec(memory_space=pl.ANY),
        scratch_shapes=scratch,
        compiler_params=pltpu.CompilerParams(
            collective_id=0, has_side_effects=True, vmem_limit_bytes=60 * 2**20
        ),
        name="backward_messages",
    )(feature_u, feature_v, emission, word_ids, scales, backward_end)


def solution(mesh):
    placed = (
        P("state", "seq"),
        P("state", "seq"),
        P("seq", "state"),
        P(),
        P("seq", None),
        P("seq", "state"),
    )
    return jax.shard_map(
        body, mesh=mesh, in_specs=placed, out_specs=P(None, "seq", "state"), check_vma=False
    )
```
